256 devices in a mesh: dp: 4 (over x_lo, core), col: 64 (over y, z, x_hi).
Axes of the slice: x: 4 (x_hi: 2, x_lo: 2; x = x_hi * 2 + x_lo), y: 4, z: 8, core: 2. Of those that a mesh axis runs over, the one named last changes fastest.
Arguments:
- proj: bfloat16 [8192, 2048], P('col', 'dp'), may hold values from -0.0625 to 0.0625
- mean: float32 [8192], P('col'), may hold values from -0.75 to 0.75
- root: bfloat16 [8192, 8192], P(None, 'col'), may hold values from -0.1875 to 0.1875
- resid_var: float32 [2048], P('dp'), may hold values from 0.05 to 1
- targets: float32 [65536], replicated, may hold values from -8 to 8
- indices: int32 [2048], P('dp'), may hold values from 0 to 65535
Outputs:
- grad_mean: float32 [8192], P('col')
- grad_root: float32 [8192, 8192], P('dp', 'col')
- grad_proj: float32 [8192, 2048], P('col', 'dp')
The draws below stay inside these ranges and needn't reach their ends.
All inputs are finite; a program needn't handle non-finite values.
Results may differ from the reference program's by a relative error of at most 0.0026.
Values may be sent and summed in bfloat16 or wider, within the bound.
A program may use at most 64 MiB of HBM per device.

```python
import math
import jax
import jax.numpy as jnp
import numpy as np
from jax import lax

M = 8192
WINDOW = 65536
ROWS = 2048


def place_ends(drawn, own_key, low, high):
    longest = drawn.shape.index(max(drawn.shape))
    spots = []
    for shift in (0, 1):
        where = [jax.random.randint(jax.random.fold_in(own_key, axis), (), 0, length) for axis, length in enumerate(drawn.shape)]
        where[longest] = (where[longest] + shift) % drawn.shape[longest]
        spots.append(tuple(where))
    return drawn.at[spots[0]].set(low).at[spots[1]].set(high)


def strengthened(drawn, stream_key, source, target, shards_of, factor):
    def block_of(dim):
        return (jnp.arange(drawn.shape[dim]) // (drawn.shape[dim] // shards_of)).reshape((-1,) + (1,) * (drawn.ndim - 1 - dim))

    one_side = jax.random.permutation(stream_key, shards_of)[block_of(target)]
    far = (block_of(target) + shards_of // 2) % shards_of
    return jnp.where((block_of(source) == one_side) | (block_of(source) == far), factor * drawn, drawn)


def steps_of(key, dims, split, least, top_value):
    factor_of = 1.0
    for dim, blocks in split:
        steps = jax.random.uniform(jax.random.fold_in(jax.random.fold_in(key, 6), dim), (blocks,), jnp.float32, least / len(split), top_value / len(split))
        factor_of = factor_of * jnp.repeat(jnp.exp(steps), dims[dim] // blocks).reshape((-1,) + (1,) * (len(dims) - 1 - dim))
    return factor_of


def gaussian(stream_key, extent, spread, reach, shards=(), held_as=jnp.bfloat16):
    loudness = steps_of(stream_key, extent, shards, -0.22, 0.18) if shards else 1.0
    values = jax.random.normal(stream_key, extent, jnp.float32) * spread * loudness
    return jnp.minimum(jnp.maximum(values, -reach), reach).astype(held_as)


def noise_with(key, shape, width, limit, pieces, heavy, kind=jnp.bfloat16):
    drawn = width * jax.random.normal(key, shape, jnp.float32)
    if pieces:
        drawn = drawn * steps_of(key, shape, pieces, -0.22, 0.18)
    return jnp.clip(strengthened(drawn, jax.random.fold_in(key, 3), *heavy), -limit, limit).astype(kind)


def setup_inputs(seed: int = 0) -> dict:
    arg_keys = jax.random.split(jax.random.key(seed), 7)
    proj = gaussian(arg_keys[0], (M, ROWS), M ** -0.5, 0.0625, ((0, 64), (1, 4)))
    mean = gaussian(arg_keys[1], (M,), 0.05, 0.75, ((0, 64),), jnp.float32)
    root = noise_with(arg_keys[2], (M, M), M ** -0.5, 0.1875, ((1, 64),), (1, 0, 64, 4.0))
    resid_var = jnp.clip(jnp.exp(math.log(1.0) - 2.9957323 * jax.random.uniform(arg_keys[3], (ROWS,), jnp.float32) ** steps_of(arg_keys[3], (ROWS,), ((0, 4),), -0.2, 0.2)), 0.05, 1.0)
    targets = gaussian(arg_keys[4], (WINDOW,), 1.5, 8.0, (), jnp.float32)
    indices = place_ends(jax.random.randint(arg_keys[5], (ROWS,), 0, WINDOW), jax.random.fold_in(arg_keys[5], 1), 0, WINDOW - 1).astype(jnp.int32)
    return {"proj": proj, "mean": mean, "root": root, "resid_var": resid_var, "targets": targets, "indices": indices}


freedom = 4.0
half_knots = [0.2453407083009012, 0.7374737285453944, 1.234076215395323, 1.7385377121165861, 2.2549740020892757, 2.7888060584281305, 3.3478545673832163, 3.944764040115625, 4.603682449550744, 5.387480890011233]
half_weights = [0.4622436696006101, 0.2866755053628341, 0.1090172060200233, 0.024810520887463612, 0.0032437733422378567, 0.00022833863601635319, 7.802556478532063e-06, 1.0860693707692819e-07, 4.3993409922731804e-10, 2.2293936455341508e-13]

def hermite_table():
    positive = np.array(half_knots)
    heights = np.array(half_weights)
    knots = np.concatenate([-positive[::-1], positive])
    weights = np.concatenate([heights[::-1], heights])
    return (knots, weights)

def expected_slopes(observed, post_mean, post_var):
    knots, weights = hermite_table()
    knots = jnp.asarray(knots, jnp.float32)[:, None]
    weights = jnp.asarray(weights / np.sqrt(np.pi), jnp.float32)[:, None]
    spread_root = jnp.sqrt(2.0 * post_var)
    values = post_mean[None, :] + spread_root[None, :] * knots
    gap = observed[None, :] - values
    slope = (freedom + 1.0) * gap / (freedom + gap * gap)
    factor = WINDOW / ROWS
    slope_mean = factor * lax.optimization_barrier(jnp.sum(weights * slope, axis=0))
    slope_var = factor * lax.optimization_barrier(jnp.sum(weights * slope * knots, axis=0)) / spread_root
    return (slope_mean, slope_var)

def reference(proj, mean, root, resid_var, targets, indices):
    observed = jnp.take(targets, indices.astype(jnp.int32))
    latent = jnp.dot(root.T, proj, preferred_element_type=jnp.float32)
    post_mean = jnp.dot(mean, proj.astype(jnp.float32), precision=lax.Precision.HIGHEST)
    post_var = resid_var + lax.optimization_barrier(jnp.sum(latent * latent, axis=0))
    slope_mean, slope_var = expected_slopes(observed, post_mean, post_var)
    weighted = (2.0 * slope_var[None, :] * latent).astype(jnp.bfloat16)
    grad_mean = jnp.dot(proj.astype(jnp.float32), slope_mean, precision=lax.Precision.HIGHEST)
    grad_root = jnp.dot(proj, weighted.T, preferred_element_type=jnp.float32)
    grad_proj = mean[:, None] * slope_mean[None, :] + jnp.dot(root, weighted, preferred_element_type=jnp.float32)
    return (grad_mean, grad_root, grad_proj)
```

```python
import functools

import jax
import jax.numpy as jnp
import numpy as np
from jax import lax
from jax.experimental import pallas as pl
from jax.experimental.pallas import tpu as pltpu
from jax.sharding import PartitionSpec as P

WINDOW = 65536
ROWS = 2048
MESH = pl.DeviceIdType.MESH
F32 = jnp.float32
BF16 = jnp.bfloat16
HIGHEST = lax.Precision.HIGHEST

freedom = 4.0
half_knots = [
    0.2453407083009012,
    0.7374737285453944,
    1.234076215395323,
    1.7385377121165861,
    2.2549740020892757,
    2.7888060584281305,
    3.3478545673832163,
    3.944764040115625,
    4.603682449550744,
    5.387480890011233,
]
half_weights = [
    0.4622436696006101,
    0.2866755053628341,
    0.1090172060200233,
    0.024810520887463612,
    0.0032437733422378567,
    0.00022833863601635319,
    7.802556478532063e-06,
    1.0860693707692819e-07,
    4.3993409922731804e-10,
    2.2293936455341508e-13,
]


def slopes(observed, post_mean, post_var):
    knots = [-k for k in half_knots[::-1]] + half_knots
    weights = half_weights[::-1] + half_weights
    spread_root = jnp.sqrt(2.0 * post_var)
    total_mean = jnp.zeros_like(observed)
    total_var = jnp.zeros_like(observed)
    for knot, weight in zip(knots, weights):
        knot = float(np.float32(knot))
        weight = float(np.float32(weight / np.sqrt(np.pi)))
        gap = observed - (post_mean + spread_root * knot)
        term = weight * ((freedom + 1.0) * gap / (freedom + gap * gap))
        total_mean = total_mean + term
        total_var = total_var + term * knot
    factor = WINDOW / ROWS
    return factor * total_mean, factor * total_var / spread_root


def kernel(
    proj, mean, root, resid, table, index,
    out_mean, out_root, out_proj,
    rootb, projb, lat_out, lat_in, wb, grp, grc, gin, gpo, gpi,
    ar_src, ar_z, ar_p_src, ar_p, gm_src, gm_in,
    local_sem, root_ss, root_rs, half_ss, half_rs, z_ss, z_rs,
    lat_ss, lat_rs, az_ss, az_rs, ap_ss, ap_rs, w_ss, w_rs,
    c_ss, c_rs, g_ss, g_rs, gp_ss, gp_rs, gm_ss, gm_rs,
):
    d = lax.axis_index("dp")
    col = lax.axis_index("col")
    xl, core = d // 2, d % 2
    y, z, xh = col // 16, (col // 2) % 8, col % 2
    p = y * 2 + xh
    other = xl * 2 + (1 - core)

    def column(y_, z_, xh_):
        return y_ * 16 + z_ * 2 + xh_

    def p_to(j):
        return ((y + j // 2) % 4) * 2 + (xh + j % 2) % 2

    def p_from(j):
        return ((y + 4 - j // 2) % 4) * 2 + (xh + 2 - j % 2) % 2

    def p_dev(q):
        return (d, column(q // 2, z, q % 2))

    def z_to(j):
        return (z + j) % 8

    def z_from(j):
        return (z + 8 - j) % 8

    def z_dev(q):
        return (d, column(y, q, xh))

    def copy(src, dst, ss, rs, dev):
        return pltpu.make_async_remote_copy(
            src_ref=src, dst_ref=dst, send_sem=ss, recv_sem=rs,
            device_id=dev, device_id_type=MESH,
        )

    def loop(lo, hi, body):
        def step(j, carry):
            body(j)
            return carry
        lax.fori_loop(lo, hi, step, 0)

    to_d = y
    self_gr = to_d == d

    def g_from_dev(s):
        return (s // 2, column(d, z, s % 2))

    barrier = pltpu.get_barrier_semaphore()

    def greet(dev):
        pl.semaphore_signal(barrier, inc=1, device_id=dev, device_id_type=MESH)

    loop(1, 8, lambda j: greet(p_dev(p_from(j))))
    loop(1, 8, lambda j: greet(z_dev(z_from(j))))
    loop(1, 4, lambda j: greet(((d + j) % 4, col)))
    me_gr = d * 2 + xh

    def greet_gr(s):
        @pl.when(jnp.logical_not(jnp.logical_and(self_gr, s == me_gr)))
        def _():
            greet(g_from_dev(s))

    loop(0, 8, greet_gr)
    pl.semaphore_wait(barrier, 7 + 7 + 3 + 8 - jnp.where(self_gr, 1, 0))

    def proj_copy(j, q_to, q_from):
        return copy(proj, projb.at[z], z_ss.at[j], z_rs.at[j], z_dev(q_to))

    def start_z(j):
        copy(proj, projb.at[z], z_ss.at[j], z_rs.at[j], z_dev(z_to(j))).start()

    half = pl.ds(core * 4, 4)

    def cols(q):
        return pl.ds(pl.multiple_of(q * 128, 128), 128)

    def start_root(j):
        q = p_to(j)
        copy(
            root.at[q // 2, half, q % 2], rootb.at[half, :, cols(p)],
            root_ss.at[j], root_rs.at[j], p_dev(q),
        ).start()

    loop(1, 8, start_z)
    loop(1, 8, start_root)
    own_root = pltpu.make_async_copy(root.at[y, half, xh], rootb.at[half, :, cols(p)], local_sem)
    own_root.start()
    projb[z] = proj[...]

    mean_rows = jnp.broadcast_to(mean[...], (8, 128))
    part_mean = jnp.dot(
        mean_rows, proj[...].astype(F32), precision=HIGHEST, preferred_element_type=F32
    )
    ar_src[:, 512:] = part_mean[0:1]
    picked = []
    for part in range(4):
        idx = index[:, part * 128 : (part + 1) * 128]
        row, lane = idx // 128, idx % 128
        chosen = jnp.where(lax.broadcasted_iota(jnp.int32, (512, 128), 0) == row, 1.0, 0.0)
        values = lax.dot_general(
            table[...], chosen, (((0,), (0,)), ((), ())),
            precision=HIGHEST, preferred_element_type=F32,
        )
        here = lax.broadcasted_iota(jnp.int32, (128, 128), 0) == lane
        picked.append(jnp.sum(jnp.where(here, values, 0.0), axis=0, keepdims=True))
    observed = jnp.concatenate(picked, axis=1)

    own_root.wait()

    def wait_root(j):
        q = p_from(j)
        copy(
            root.at[y, half, xh], rootb.at[half, :, cols(q)],
            root_ss.at[j], root_rs.at[j], p_dev(q),
        ).wait_recv()

    loop(1, 8, wait_root)
    share = copy(rootb.at[half], rootb.at[half], half_ss, half_rs, (other, col))
    share.start()

    def wait_z(j):
        q = z_from(j)
        copy(proj, projb.at[q], z_ss.at[j], z_rs.at[j], z_dev(q)).wait_recv()

    loop(1, 8, wait_z)
    other_half = pl.ds((1 - core) * 4, 4)
    copy(rootb.at[other_half], rootb.at[other_half], half_ss, half_rs, (other, col)).wait_recv()

    def latent_piece(q):
        block = rootb[:, :, cols(q)].reshape(1024, 128)
        return lax.dot_general(
            block, projb[...].reshape(1024, 512), (((0,), (0,)), ((), ())),
            preferred_element_type=F32,
        )

    def lat_copy(j, q, slot):
        return copy(lat_out.at[j], lat_in.at[slot], lat_ss.at[j], lat_rs.at[j], p_dev(q))

    def send_lat(j):
        q = p_to(j)
        lat_out[j] = latent_piece(q)
        lat_copy(j, q, p).start()

    loop(1, 8, send_lat)
    lat_in[p] = latent_piece(p)

    def wait_lat(j):
        q = p_from(j)
        lat_copy(j, q, q).wait_recv()

    loop(1, 8, wait_lat)
    latent = lat_in[0]
    for i in range(1, 8):
        latent = latent + lat_in[i]
    lat_in[0] = latent
    ar_src[:, :512] = jnp.sum(latent * latent, axis=0, keepdims=True)

    def az_copy(j, q, slot):
        return copy(ar_src, ar_z.at[slot], az_ss.at[j], az_rs.at[j], z_dev(q))

    loop(1, 8, lambda j: az_copy(j, z_to(j), z).start())
    ar_z[z] = ar_src[...]
    loop(1, 8, lambda j: az_copy(j, z_from(j), z_from(j)).wait_recv())
    total = ar_z[0]
    for i in range(1, 8):
        total = total + ar_z[i]
    ar_p_src[...] = total

    def ap_copy(j, q, slot):
        return copy(ar_p_src, ar_p.at[slot], ap_ss.at[j], ap_rs.at[j], p_dev(q))

    loop(1, 8, lambda j: ap_copy(j, p_to(j), p).start())
    ar_p[p] = total
    loop(1, 8, lambda j: ap_copy(j, p_from(j), p_from(j)).wait_recv())
    total = ar_p[0]
    for i in range(1, 8):
        total = total + ar_p[i]
    post_var = resid[...] + total[:, :512]
    post_mean = total[:, 512:]
    slope_mean, slope_var = slopes(observed, post_mean, post_var)

    wb[p] = (2.0 * slope_var * lat_in[0]).astype(BF16)

    def w_copy(j, q, slot):
        return copy(wb.at[p], wb.at[slot], w_ss.at[j], w_rs.at[j], p_dev(q))

    loop(1, 8, lambda j: w_copy(j, p_to(j), p).start())

    gm = lax.dot_general(
        jnp.broadcast_to(slope_mean, (8, 512)), proj[...].astype(F32),
        (((1,), (1,)), ((), ())), precision=HIGHEST, preferred_element_type=F32,
    )
    gm_src[...] = gm[0:1]
    gm_in[d] = gm[0:1]

    def gm_copy(j, e, slot):
        return copy(gm_src, gm_in.at[slot], gm_ss.at[j], gm_rs.at[j], (e, col))

    loop(1, 4, lambda j: gm_copy(j, (d + j) % 4, d).start())

    own_rows = pl.ds(pl.multiple_of(core * 512, 512), 512)
    other_rows = pl.ds(pl.multiple_of((1 - core) * 512, 512), 512)

    def c_copy(j, q, rows_):
        return copy(grp.at[q, rows_], grc.at[q], c_ss.at[j], c_rs.at[j], (other, col))

    def root_piece(j):
        q = p_from(j)

        @pl.when(j > 0)
        def _():
            w_copy(j, q, q).wait_recv()

        grp[q] = lax.dot_general(
            projb[...].reshape(1024, 512), wb[q], (((1,), (1,)), ((), ())),
            preferred_element_type=F32,
        )
        c_copy(j, q, other_rows).start()

    loop(0, 8, root_piece)

    def gp_copy(j, q, slot):
        return copy(gpo.at[j], gpi.at[slot], gp_ss.at[j], gp_rs.at[j], z_dev(q))

    def proj_piece(q):
        return jnp.dot(rootb[q], wb[...].reshape(1024, 512), preferred_element_type=F32)

    def send_gp(j):
        q = z_to(j)
        gpo[j] = proj_piece(q).astype(BF16)
        gp_copy(j, q, z).start()

    loop(1, 8, send_gp)

    def g_copy(j, q):
        return copy(
            grp.at[q, own_rows], gin.at[me_gr], g_ss.at[j], g_rs.at[me_gr],
            (to_d, column(q // 2, z, q % 2)),
        )

    def send_gr(j):
        q = p_from(j)
        c_copy(j, q, other_rows).wait_recv()
        grp[q, own_rows] = grp[q, own_rows] + grc[q]
        mine = jnp.logical_and(self_gr, j == 0)

        @pl.when(mine)
        def _():
            pltpu.make_async_copy(grp.at[q, own_rows], gin.at[me_gr], g_rs.at[me_gr]).start()

        @pl.when(jnp.logical_not(mine))
        def _():
            g_copy(j, q).start()

    loop(0, 8, send_gr)

    own = proj_piece(z) + jnp.transpose(mean_rows)[:, 0:1] * slope_mean
    loop(1, 4, lambda j: gm_copy(j, (d + 4 - j) % 4, (d + 4 - j) % 4).wait_recv())
    out_mean[...] = gm_in[0] + gm_in[1] + gm_in[2] + gm_in[3]

    loop(1, 8, lambda j: gp_copy(j, z_from(j), z_from(j)).wait_recv())
    out_proj[...] = own

    def add_gp(j):
        out_proj[...] += gpi[z_from(j)].astype(F32)

    loop(1, 8, add_gp)

    def wait_gr(s):
        pltpu.make_async_copy(gin.at[s], gin.at[s], g_rs.at[s]).wait()

    loop(0, 8, wait_gr)
    for k in range(2):
        for h in range(2):
            block = gin[k * 2 + h] + gin[4 + k * 2 + h]
            out_root[k * 4 : k * 4 + 4, h] = block.reshape(4, 128, 128)

    def drain(j):
        z_copy = copy(proj, projb.at[z], z_ss.at[j], z_rs.at[j], z_dev(z_to(j)))
        z_copy.wait_send()
        q = p_to(j)
        copy(
            root.at[q // 2, half, q % 2], rootb.at[half, :, cols(p)],
            root_ss.at[j], root_rs.at[j], p_dev(q),
        ).wait_send()
        lat_copy(j, q, p).wait_send()
        az_copy(j, z_to(j), z).wait_send()
        ap_copy(j, q, p).wait_send()
        w_copy(j, q, p).wait_send()
        gp_copy(j, z_to(j), z).wait_send()

    loop(1, 8, drain)
    share.wait_send()
    loop(1, 4, lambda j: gm_copy(j, (d + j) % 4, d).wait_send())

    def drain_gr(j):
        q = p_from(j)
        c_copy(j, q, other_rows).wait_send()

        @pl.when(jnp.logical_not(jnp.logical_and(self_gr, j == 0)))
        def _():
            g_copy(j, q).wait_send()

    loop(0, 8, drain_gr)


def on_device(proj, mean, root, resid_var, targets, indices):
    vmem = pl.BlockSpec(memory_space=pltpu.VMEM)
    sem = pltpu.SemaphoreType.DMA
    out_mean, out_root, out_proj = pl.pallas_call(
        kernel,
        out_shape=(
            jax.ShapeDtypeStruct((1, 128), F32),
            jax.ShapeDtypeStruct((8, 2, 128, 128), F32),
            jax.ShapeDtypeStruct((128, 512), F32),
        ),
        in_specs=[vmem, vmem, pl.BlockSpec(memory_space=pl.ANY), vmem, vmem, vmem],
        out_specs=(vmem, vmem, vmem),
        scratch_shapes=[
            pltpu.VMEM((8, 128, 1024), BF16),
            pltpu.VMEM((8, 128, 512), BF16),
            pltpu.VMEM((8, 128, 512), F32),
            pltpu.VMEM((8, 128, 512), F32),
            pltpu.VMEM((8, 128, 512), BF16),
            pltpu.VMEM((8, 1024, 128), F32),
            pltpu.VMEM((8, 512, 128), F32),
            pltpu.VMEM((8, 512, 128), F32),
            pltpu.VMEM((8, 128, 512), BF16),
            pltpu.VMEM((8, 128, 512), BF16),
            pltpu.VMEM((1, 1024), F32),
            pltpu.VMEM((8, 1, 1024), F32),
            pltpu.VMEM((1, 1024), F32),
            pltpu.VMEM((8, 1, 1024), F32),
            pltpu.VMEM((1, 128), F32),
            pltpu.VMEM((4, 1, 128), F32),
            sem,
            sem((8,)), sem((8,)), sem, sem, sem((8,)), sem((8,)),
            sem((8,)), sem((8,)), sem((8,)), sem((8,)), sem((8,)), sem((8,)),
            sem((8,)), sem((8,)),
            sem((8,)), sem((8,)), sem((8,)), sem((8,)), sem((8,)), sem((8,)),
            sem((4,)), sem((4,)),
        ],
        compiler_params=pltpu.CompilerParams(
            collective_id=0, has_side_effects=True, vmem_limit_bytes=48 * 2**20
        ),
    )(
        proj,
        mean.reshape(1, 128),
        root.reshape(4, 8, 2, 128, 128),
        resid_var.reshape(1, 512),
        targets.reshape(512, 128),
        indices.reshape(1, 512),
    )
    return out_mean.reshape(128), out_root.reshape(2048, 128), out_proj


def solution(mesh):
    return jax.shard_map(
        on_device,
        mesh=mesh,
        in_specs=(P("col", "dp"), P("col"), P(None, "col"), P("dp"), P(), P("dp")),
        out_specs=(P("col"), P("dp", "col"), P("col", "dp")),
        check_vma=False,
    )
```

```python
import functools

import jax
import jax.numpy as jnp
import numpy as np
from jax import lax
from jax.experimental import pallas as pl
from jax.experimental.pallas import tpu as pltpu
from jax.sharding import PartitionSpec as P

WINDOW = 65536
ROWS = 2048
MESH = pl.DeviceIdType.MESH
NH = 2
N = 512 // NH
F32 = jnp.float32
BF16 = jnp.bfloat16
HIGHEST = lax.Precision.HIGHEST

freedom = 4.0
half_knots = [
    0.2453407083009012,
    0.7374737285453944,
    1.234076215395323,
    1.7385377121165861,
    2.2549740020892757,
    2.7888060584281305,
    3.3478545673832163,
    3.944764040115625,
    4.603682449550744,
    5.387480890011233,
]
half_weights = [
    0.4622436696006101,
    0.2866755053628341,
    0.1090172060200233,
    0.024810520887463612,
    0.0032437733422378567,
    0.00022833863601635319,
    7.802556478532063e-06,
    1.0860693707692819e-07,
    4.3993409922731804e-10,
    2.2293936455341508e-13,
]


def slopes(observed, post_mean, post_var):
    knots = [-k for k in half_knots[::-1]] + half_knots
    weights = half_weights[::-1] + half_weights
    spread_root = jnp.sqrt(2.0 * post_var)
    total_mean = jnp.zeros_like(observed)
    total_var = jnp.zeros_like(observed)
    for knot, weight in zip(knots, weights):
        knot = float(np.float32(knot))
        weight = float(np.float32(weight / np.sqrt(np.pi)))
        gap = observed - (post_mean + spread_root * knot)
        term = weight * ((freedom + 1.0) * gap / (freedom + gap * gap))
        total_mean = total_mean + term
        total_var = total_var + term * knot
    factor = WINDOW / ROWS
    return factor * total_mean, factor * total_var / spread_root


def kernel(
    proj_hbm, mean_hbm, root, resid_hbm, table_hbm, index_hbm,
    out_mean, out_root, out_proj,
    proj, mean, resid, table, index, in_sem,
    rootb, projb, lat_out, lat_in, wb, grp, grc, gout, gin, gpo, gpi,
    ar_src, ar_z, ar_p_src, ar_p, gm_src, gm_in,
    local_sem, root_ss, root_rs, half_ss, half_rs, z_ss, z_rs,
    lat_ss, lat_rs, az_ss, az_rs, ap_ss, ap_rs, w_ss, w_rs,
    c_ss, c_rs, g_ss, g_rs, gp_ss, gp_rs, gm_ss, gm_rs,
):
    d = lax.axis_index("dp")
    col = lax.axis_index("col")
    core = d % 2
    y, z, xh = col // 16, (col // 2) % 8, col % 2
    p = y * 2 + xh
    other = d + 1 - 2 * core

    def column(y_, z_, xh_):
        return y_ * 16 + z_ * 2 + xh_

    def p_to(j):
        return ((y + j // 2) % 4) * 2 + (xh + j % 2) % 2

    def p_from(j):
        return ((y + 4 - j // 2) % 4) * 2 + (xh + 2 - j % 2) % 2

    def p_dev(q):
        return (d, column(q // 2, z, q % 2))

    def z_to(j):
        return (z + j) % 8

    def z_from(j):
        return (z + 8 - j) % 8

    def z_dev(q):
        return (d, column(y, q, xh))

    def copy(src, dst, ss, rs, dev):
        return pltpu.make_async_remote_copy(
            src_ref=src, dst_ref=dst, send_sem=ss, recv_sem=rs,
            device_id=dev, device_id_type=MESH,
        )

    def loop(lo, hi, body):
        def step(j, carry):
            body(j)
            return carry
        lax.fori_loop(lo, hi, step, 0)

    incoming = [
        pltpu.make_async_copy(a, b, in_sem.at[i])
        for i, (a, b) in enumerate(
            [
                (proj_hbm, proj), (mean_hbm, mean), (index_hbm, index),
                (table_hbm, table), (resid_hbm, resid),
            ]
        )
    ]
    for item in incoming:
        item.start()

    def cols(q):
        return pl.ds(pl.multiple_of(q * 128, 128), 128)

    own_root = pltpu.make_async_copy(root.at[y, :, xh], rootb.at[:, :, cols(p)], local_sem)
    own_root.start()

    self_gr = y == d
    me_gr = d * 2 + xh

    barrier = pltpu.get_barrier_semaphore()

    def greet(dev):
        pl.semaphore_signal(barrier, inc=1, device_id=dev, device_id_type=MESH)

    greet(z_dev(z_to(1)))
    greet(z_dev(z_from(1)))
    loop(1, 8, lambda j: greet(p_dev(p_from(j))))
    loop(1, 4, lambda j: greet(((d + j) % 4, col)))
    pl.semaphore_wait(barrier, 2 + 7 + 3)

    def part(zz, c):
        if NH == 2:
            return projb.at[c, zz]
        return projb.at[0, zz, :, c * 256 : (c + 1) * 256]

    def ring(way, step, c):
        zz = (z + 8 - way * (step - 1)) % 8
        src = proj.at[:, c * 256 : (c + 1) * 256] if step == 1 else part(zz, c)
        i = (0 if way == 1 else 1) * 2 + c
        return copy(src, part(zz, c), z_ss.at[i, step], z_rs.at[i, step], z_dev((z + 8 + way) % 8))

    def ring_wait(way, step, c):
        zz = (z + 8 - way * step) % 8
        i = (0 if way == 1 else 1) * 2 + c
        copy(part(zz, c), part(zz, c), z_ss.at[i, step], z_rs.at[i, step], z_dev((z + 8 + way) % 8)).wait_recv()

    def goes(way, step, c):
        return step < 4 or (c == 0) == (way == 1)

    half = pl.ds(core * 4, 4)
    other_half = pl.ds((1 - core) * 4, 4)

    def root_copy(j):
        q = p_to(j)
        return copy(
            root.at[q // 2, half, q % 2], rootb.at[half, :, cols(p)],
            root_ss.at[j], root_rs.at[j], p_dev(q),
        )

    incoming[0].wait()
    for c in range(2):
        for way in (1, -1):
            ring(way, 1, c).start()
    loop(1, 8, lambda j: root_copy(j).start())
    for h in range(NH):
        projb[h, z] = proj[:, h * N : (h + 1) * N]
    for item in incoming[1:]:
        item.wait()

    mean_rows = jnp.broadcast_to(mean[...], (8, 128))
    part_mean = jnp.dot(
        mean_rows, proj[...].astype(F32), precision=HIGHEST, preferred_element_type=F32
    )
    for h in range(NH):
        ar_src[h, :, N:] = part_mean[0:1, h * N : (h + 1) * N]
    picked = []
    for i in range(4):
        idx = index[:, i * 128 : (i + 1) * 128]
        row, lane = idx // 128, idx % 128
        chosen = jnp.where(lax.broadcasted_iota(jnp.int32, (512, 128), 0) == row, 1.0, 0.0)
        values = lax.dot_general(
            table[...], chosen, (((0,), (0,)), ((), ())),
            precision=HIGHEST, preferred_element_type=F32,
        )
        here = lax.broadcasted_iota(jnp.int32, (128, 128), 0) == lane
        picked.append(jnp.sum(jnp.where(here, values, 0.0), axis=0, keepdims=True))
    observed = jnp.concatenate(picked, axis=1)

    for step in range(2, 5):
        for c in range(2):
            for way in (1, -1):
                ring_wait(way, step - 1, c)
                if goes(way, step, c):
                    ring(way, step, c).start()

    def share_root(j):
        q = p_from(j)
        copy(
            root.at[y, half, xh], rootb.at[half, :, cols(q)],
            root_ss.at[j], root_rs.at[j], p_dev(q),
        ).wait_recv()
        share_copy(j, half).start()

    def share_copy(j, rows_):
        block = rootb.at[rows_, :, cols(p_from(j))]
        return copy(block, block, half_ss.at[j], half_rs.at[j], (other, col))

    loop(1, 8, share_root)
    ring_wait(1, 4, 0)
    ring_wait(-1, 4, 1)
    own_root.wait()
    loop(1, 8, lambda j: share_copy(j, other_half).wait_recv())

    def latent_piece(h, q):
        block = rootb[:, :, cols(q)].reshape(1024, 128)
        return lax.dot_general(
            block, projb[h].reshape(1024, N), (((0,), (0,)), ((), ())),
            preferred_element_type=F32,
        )

    def lat_copy(h, j, q, slot):
        return copy(
            lat_out.at[h, j], lat_in.at[h, slot], lat_ss.at[h, j], lat_rs.at[h, j], p_dev(q)
        )

    def send_latent(h):
        def body(j):
            q = p_to(j)
            lat_out[h, j] = latent_piece(h, q)
            lat_copy(h, j, q, p).start()

        loop(1, 8, body)
        lat_in[h, p] = latent_piece(h, p)

    def az_copy(h, j, q, slot):
        return copy(ar_src.at[h], ar_z.at[h, slot], az_ss.at[h, j], az_rs.at[h, j], z_dev(q))

    def ap_copy(h, j, q, slot):
        return copy(ar_p_src.at[h], ar_p.at[h, slot], ap_ss.at[h, j], ap_rs.at[h, j], p_dev(q))

    def sum_latent(h):
        def body(j):
            q = p_from(j)
            lat_copy(h, j, q, q).wait_recv()

        loop(1, 8, body)
        latent = lat_in[h, 0]
        for i in range(1, 8):
            latent = latent + lat_in[h, i]
        lat_in[h, 0] = latent
        ar_src[h, :, :N] = jnp.sum(latent * latent, axis=0, keepdims=True)
        loop(1, 8, lambda j: az_copy(h, j, z_to(j), z).start())
        ar_z[h, z] = ar_src[h]

    def sum_along_z(h):
        loop(1, 8, lambda j: az_copy(h, j, z_from(j), z_from(j)).wait_recv())
        total = ar_z[h, 0]
        for i in range(1, 8):
            total = total + ar_z[h, i]
        ar_p_src[h] = total
        loop(1, 8, lambda j: ap_copy(h, j, p_to(j), p).start())
        ar_p[h, p] = total

    def w_copy(h, j, q, slot):
        return copy(wb.at[h, p], wb.at[h, slot], w_ss.at[h, j], w_rs.at[h, j], p_dev(q))

    def send_weighted(h):
        loop(1, 8, lambda j: ap_copy(h, j, p_from(j), p_from(j)).wait_recv())
        total = ar_p[h, 0]
        for i in range(1, 8):
            total = total + ar_p[h, i]
        rows_ = slice(h * N, (h + 1) * N)
        post_var = resid[:, rows_] + total[:, :N]
        slope_mean, slope_var = slopes(observed[:, rows_], total[:, N:], post_var)
        wb[h, p] = (2.0 * slope_var * lat_in[h, 0]).astype(BF16)
        loop(1, 8, lambda j: w_copy(h, j, p_to(j), p).start())
        return slope_mean

    own_rows = pl.ds(pl.multiple_of(core * 512, 512), 512)
    other_rows = pl.ds(pl.multiple_of((1 - core) * 512, 512), 512)

    def c_copy(j, q, rows_):
        return copy(grp.at[q, rows_], grc.at[q], c_ss.at[j], c_rs.at[j], (other, col))

    def root_pieces(h):
        def body(j):
            q = p_from(j)

            @pl.when(j > 0)
            def _():
                w_copy(h, j, q, q).wait_recv()

            piece = lax.dot_general(
                projb[h].reshape(1024, N), wb[h, q], (((1,), (1,)), ((), ())),
                preferred_element_type=F32,
            )
            if h == 0:
                grp[q] = piece
            else:
                grp[q] += piece
            if h == NH - 1:
                c_copy(j, q, other_rows).start()

        loop(0, 8, body)

    def gp_copy(h, j, q, slot):
        return copy(gpo.at[h, j], gpi.at[h, slot], gp_ss.at[h, j], gp_rs.at[h, j], z_dev(q))

    def proj_piece(h, q):
        return jnp.dot(rootb[q], wb[h].reshape(1024, N), preferred_element_type=F32)

    def proj_pieces(h):
        def body(j):
            q = z_to(j)
            gpo[h, j] = proj_piece(h, q).astype(BF16)
            gp_copy(h, j, q, z).start()

        loop(1, 8, body)

    if NH == 1:
        send_latent(0)
        sum_latent(0)
        sum_along_z(0)
        slope_mean = send_weighted(0)
    else:
        send_latent(0)
        send_latent(1)
        sum_latent(0)
        sum_along_z(0)
        first = send_weighted(0)
        sum_latent(1)
        sum_along_z(1)
        root_pieces(0)
        second = send_weighted(1)
        proj_pieces(0)
        slope_mean = jnp.concatenate([first, second], axis=1)

    gm = lax.dot_general(
        jnp.broadcast_to(slope_mean, (8, 512)), proj[...].astype(F32),
        (((1,), (1,)), ((), ())), precision=HIGHEST, preferred_element_type=F32,
    )
    gm_src[...] = gm[0:1]
    gm_in[d] = gm[0:1]

    def gm_copy(j, e, slot):
        return copy(gm_src, gm_in.at[slot], gm_ss.at[j], gm_rs.at[j], (e, col))

    loop(1, 4, lambda j: gm_copy(j, (d + j) % 4, d).start())
    root_pieces(NH - 1)
    proj_pieces(NH - 1)

    def g_copy(j, q):
        return copy(
            gout.at[q], gin.at[me_gr], g_ss.at[j], g_rs.at[me_gr],
            (y, column(q // 2, z, q % 2)),
        )

    def send_gr(j):
        q = p_from(j)
        c_copy(j, q, other_rows).wait_recv()
        gout[q] = (grp[q, own_rows] + grc[q]).astype(BF16)
        mine = jnp.logical_and(self_gr, j == 0)

        @pl.when(mine)
        def _():
            pltpu.make_async_copy(gout.at[q], gin.at[me_gr], g_rs.at[me_gr]).start()

        @pl.when(jnp.logical_not(mine))
        def _():
            g_copy(j, q).start()

    loop(0, 8, send_gr)

    outer = jnp.transpose(mean_rows)[:, 0:1] * slope_mean
    for h in range(NH):
        lat_in[h, 1] = proj_piece(h, z) + outer[:, h * N : (h + 1) * N]
    loop(1, 4, lambda j: gm_copy(j, (d + 4 - j) % 4, (d + 4 - j) % 4).wait_recv())
    out_mean[...] = gm_in[0] + gm_in[1] + gm_in[2] + gm_in[3]

    for h in range(NH):

        def add_gp(j):
            q = z_from(j)
            gp_copy(h, j, q, q).wait_recv()
            lat_in[h, 1] += gpi[h, q].astype(F32)

        loop(1, 8, add_gp)
        out_proj[:, h * N : (h + 1) * N] = lat_in[h, 1]

    def wait_gr(s):
        pltpu.make_async_copy(gin.at[s], gin.at[s], g_rs.at[s]).wait()

    loop(0, 8, wait_gr)
    for k in range(2):
        for h in range(2):
            block = gin[k * 2 + h].astype(F32) + gin[4 + k * 2 + h].astype(F32)
            out_root[k * 4 : k * 4 + 4, h] = block.reshape(4, 128, 128)

    for step in range(1, 5):
        for c in range(2):
            for way in (1, -1):
                if goes(way, step, c):
                    ring(way, step, c).wait_send()

    def drain(j):
        root_copy(j).wait_send()
        share_copy(j, half).wait_send()
        for h in range(NH):
            lat_copy(h, j, p_to(j), p).wait_send()
            az_copy(h, j, z_to(j), z).wait_send()
            ap_copy(h, j, p_to(j), p).wait_send()
            w_copy(h, j, p_to(j), p).wait_send()
            gp_copy(h, j, z_to(j), z).wait_send()

    loop(1, 8, drain)
    loop(1, 4, lambda j: gm_copy(j, (d + j) % 4, d).wait_send())

    def drain_gr(j):
        q = p_from(j)
        c_copy(j, q, other_rows).wait_send()

        @pl.when(jnp.logical_not(jnp.logical_and(self_gr, j == 0)))
        def _():
            g_copy(j, q).wait_send()

    loop(0, 8, drain_gr)


def on_device(proj, mean, root, resid_var, targets, indices):
    vmem = pl.BlockSpec(memory_space=pltpu.VMEM)
    hbm = pl.BlockSpec(memory_space=pltpu.HBM)
    sem = pltpu.SemaphoreType.DMA
    out_mean, out_root, out_proj = pl.pallas_call(
        kernel,
        out_shape=(
            jax.ShapeDtypeStruct((1, 128), F32),
            jax.ShapeDtypeStruct((8, 2, 128, 128), F32),
            jax.ShapeDtypeStruct((128, 512), F32),
        ),
        in_specs=[hbm] * 6,
        out_specs=(vmem, vmem, vmem),
        scratch_shapes=[
            pltpu.VMEM((128, 512), BF16),
            pltpu.VMEM((1, 128), F32),
            pltpu.VMEM((1, 512), F32),
            pltpu.VMEM((512, 128), F32),
            pltpu.VMEM((1, 512), jnp.int32),
            sem((5,)),
            pltpu.VMEM((8, 128, 1024), BF16),
            pltpu.VMEM((NH, 8, 128, N), BF16),
            pltpu.VMEM((NH, 8, 128, N), F32),
            pltpu.VMEM((NH, 8, 128, N), F32),
            pltpu.VMEM((NH, 8, 128, N), BF16),
            pltpu.VMEM((8, 1024, 128), F32),
            pltpu.VMEM((8, 512, 128), F32),
            pltpu.VMEM((8, 512, 128), BF16),
            pltpu.VMEM((8, 512, 128), BF16),
            pltpu.VMEM((NH, 8, 128, N), BF16),
            pltpu.VMEM((NH, 8, 128, N), BF16),
            pltpu.VMEM((NH, 1, 2 * N), F32),
            pltpu.VMEM((NH, 8, 1, 2 * N), F32),
            pltpu.VMEM((NH, 1, 2 * N), F32),
            pltpu.VMEM((NH, 8, 1, 2 * N), F32),
            pltpu.VMEM((1, 128), F32),
            pltpu.VMEM((4, 1, 128), F32),
            sem,
            sem((8,)), sem((8,)), sem((8,)), sem((8,)),
            sem((4, 5)), sem((4, 5)),
            sem((NH, 8)), sem((NH, 8)), sem((NH, 8)), sem((NH, 8)),
            sem((NH, 8)), sem((NH, 8)), sem((NH, 8)), sem((NH, 8)),
            sem((8,)), sem((8,)), sem((8,)), sem((8,)),
            sem((NH, 8)), sem((NH, 8)), sem((4,)), sem((4,)),
        ],
        compiler_params=pltpu.CompilerParams(
            collective_id=0, has_side_effects=True, vmem_limit_bytes=62 * 2**20
        ),
    )(
        proj,
        mean.reshape(1, 128),
        root.reshape(4, 8, 2, 128, 128),
        resid_var.reshape(1, 512),
        targets.reshape(512, 128),
        indices.reshape(1, 512),
    )
    return out_mean.reshape(128), out_root.reshape(2048, 128), out_proj


def solution(mesh):
    return jax.shard_map(
        on_device,
        mesh=mesh,
        in_specs=(P("col", "dp"), P("col"), P(None, "col"), P("dp"), P(), P("dp")),
        out_specs=(P("col"), P("dp", "col"), P("col", "dp")),
        check_vma=False,
    )
```

```python
import functools

import jax
import jax.numpy as jnp
import numpy as np
from jax import lax
from jax.experimental import pallas as pl
from jax.experimental.pallas import tpu as pltpu
from jax.sharding import PartitionSpec as P

WINDOW = 65536
ROWS = 2048
MESH = pl.DeviceIdType.MESH
NH = 2
N = 512 // NH
F32 = jnp.float32
BF16 = jnp.bfloat16
HIGHEST = lax.Precision.HIGHEST

freedom = 4.0
half_knots = [
    0.2453407083009012,
    0.7374737285453944,
    1.234076215395323,
    1.7385377121165861,
    2.2549740020892757,
    2.7888060584281305,
    3.3478545673832163,
    3.944764040115625,
    4.603682449550744,
    5.387480890011233,
]
half_weights = [
    0.4622436696006101,
    0.2866755053628341,
    0.1090172060200233,
    0.024810520887463612,
    0.0032437733422378567,
    0.00022833863601635319,
    7.802556478532063e-06,
    1.0860693707692819e-07,
    4.3993409922731804e-10,
    2.2293936455341508e-13,
]


def slopes(observed, post_mean, post_var):
    knots = [-k for k in half_knots[::-1]] + half_knots
    weights = half_weights[::-1] + half_weights
    spread_root = jnp.sqrt(2.0 * post_var)
    total_mean = jnp.zeros_like(observed)
    total_var = jnp.zeros_like(observed)
    for knot, weight in zip(knots, weights):
        knot = float(np.float32(knot))
        weight = float(np.float32(weight / np.sqrt(np.pi)))
        gap = observed - (post_mean + spread_root * knot)
        term = weight * ((freedom + 1.0) * gap / (freedom + gap * gap))
        total_mean = total_mean + term
        total_var = total_var + term * knot
    factor = WINDOW / ROWS
    return factor * total_mean, factor * total_var / spread_root


def kernel(
    proj_hbm, mean_hbm, root, resid_hbm, table_hbm, index_hbm,
    out_mean, out_root, out_proj,
    proj, mean, resid, table, index, in_sem,
    rootb, projb, projx, lat_out, lat_in, wb, wx, grp, gout, mid, gin, gpo, gpi,
    ar_src, ar_z, ar_p_src, ar_p, gm_src, gm_in,
    local_sem, root_ss, root_rs, half_ss, half_rs, z_ss, z_rs,
    lat_ss, lat_rs, az_ss, az_rs, ap_ss, ap_rs, w_ss, w_rs,
    px_ss, px_rs, x_ss, x_rs, m_ss, m_rs, g_ss, g_rs, gp_ss, gp_rs, gm_ss, gm_rs,
):
    d = lax.axis_index("dp")
    col = lax.axis_index("col")
    core = d % 2
    y, z, xh = col // 16, (col // 2) % 8, col % 2
    p = y * 2 + xh
    other = d + 1 - 2 * core

    def column(y_, z_, xh_):
        return y_ * 16 + z_ * 2 + xh_

    def p_to(j):
        return ((y + j // 2) % 4) * 2 + (xh + j % 2) % 2

    def p_from(j):
        return ((y + 4 - j // 2) % 4) * 2 + (xh + 2 - j % 2) % 2

    def p_dev(q):
        return (d, column(q // 2, z, q % 2))

    def z_to(j):
        return (z + j) % 8

    def z_from(j):
        return (z + 8 - j) % 8

    def z_dev(q):
        return (d, column(y, q, xh))

    def copy(src, dst, ss, rs, dev):
        return pltpu.make_async_remote_copy(
            src_ref=src, dst_ref=dst, send_sem=ss, recv_sem=rs,
            device_id=dev, device_id_type=MESH,
        )

    def loop(lo, hi, body):
        def step(j, carry):
            body(j)
            return carry
        lax.fori_loop(lo, hi, step, 0)

    incoming = [
        pltpu.make_async_copy(a, b, in_sem.at[i])
        for i, (a, b) in enumerate(
            [
                (proj_hbm, proj), (mean_hbm, mean), (index_hbm, index),
                (table_hbm, table), (resid_hbm, resid),
            ]
        )
    ]
    for item in incoming:
        item.start()

    def cols(q):
        return pl.ds(pl.multiple_of(q * 128, 128), 128)

    own_root = pltpu.make_async_copy(root.at[y, :, xh], rootb.at[:, :, cols(p)], local_sem)
    own_root.start()

    me_gr = d * 2 + xh

    barrier = pltpu.get_barrier_semaphore()

    def greet(dev):
        pl.semaphore_signal(barrier, inc=1, device_id=dev, device_id_type=MESH)

    for j in (1, 2):
        greet(z_dev(z_to(j)))
        greet(z_dev(z_from(j)))
    loop(1, 8, lambda j: greet(p_dev(p_from(j))))
    loop(1, 4, lambda j: greet(((d + j) % 4, col)))
    pl.semaphore_wait(barrier, 4 + 7 + 3)

    def part(zz, c):
        if NH == 2:
            return projb.at[c, zz]
        return projb.at[0, zz, :, c * 256 : (c + 1) * 256]

    def first(way, dist, c):
        i = (0 if way == 1 else 1) * 2 + c
        block = part(z, c)
        return copy(block, block, z_ss.at[i, dist], z_rs.at[i, dist], z_dev((z + 8 + way * dist) % 8))

    def onward(way, dist, c):
        i = (0 if way == 1 else 1) * 2 + c
        block = part((z + 8 - way * 2) % 8, c)
        return copy(block, block, z_ss.at[i, dist], z_rs.at[i, dist], z_dev((z + 8 + way * (dist - 2)) % 8))

    def goes(way, dist, c):
        return dist < 4 or (c == 0) == (way == 1)

    def arrived(way, dist, c):
        i = (0 if way == 1 else 1) * 2 + c
        block = part((z + 8 - way * dist) % 8, c)
        copy(block, block, z_ss.at[i, dist], z_rs.at[i, dist], z_dev((z + 8 + way) % 8)).wait_recv()

    def send_first(c):
        for dist in (2, 1):
            for way in (1, -1):
                first(way, dist, c).start()

    def send_onward(c):
        for way in (1, -1):
            arrived(way, 2, c)
            for dist in (4, 3):
                if goes(way, dist, c):
                    onward(way, dist, c).start()

    def all_arrived(c):
        for dist in (1, 3, 4):
            for way in (1, -1):
                if goes(way, dist, c):
                    arrived(way, dist, c)

    half = pl.ds(core * 4, 4)
    other_half = pl.ds((1 - core) * 4, 4)

    def root_copy(j):
        q = p_to(j)
        return copy(
            root.at[q // 2, half, q % 2], rootb.at[half, :, cols(p)],
            root_ss.at[j], root_rs.at[j], p_dev(q),
        )

    incoming[0].wait()
    for h in range(NH):
        projb[h, z] = proj[:, h * N : (h + 1) * N]
    send_first(0)
    loop(1, 8, lambda j: root_copy(j).start())
    send_first(1)
    for item in incoming[1:]:
        item.wait()

    mean_rows = jnp.broadcast_to(mean[...], (8, 128))
    part_mean = jnp.dot(
        mean_rows, proj[...].astype(F32), precision=HIGHEST, preferred_element_type=F32
    )
    for h in range(NH):
        ar_src[h, :, N:] = part_mean[0:1, h * N : (h + 1) * N]
    send_onward(0)
    picked = []
    for i in range(4):
        idx = index[:, i * 128 : (i + 1) * 128]
        row, lane = idx // 128, idx % 128
        chosen = jnp.where(lax.broadcasted_iota(jnp.int32, (512, 128), 0) == row, 1.0, 0.0)
        values = lax.dot_general(
            table[...], chosen, (((0,), (0,)), ((), ())),
            precision=HIGHEST, preferred_element_type=F32,
        )
        here = lax.broadcasted_iota(jnp.int32, (128, 128), 0) == lane
        picked.append(jnp.sum(jnp.where(here, values, 0.0), axis=0, keepdims=True))
    observed = jnp.concatenate(picked, axis=1)

    send_onward(1)

    def share_root(j):
        q = p_from(j)
        copy(
            root.at[y, half, xh], rootb.at[half, :, cols(q)],
            root_ss.at[j], root_rs.at[j], p_dev(q),
        ).wait_recv()
        share_copy(j, half).start()

    def share_copy(j, rows_):
        block = rootb.at[rows_, :, cols(p_from(j))]
        return copy(block, block, half_ss.at[j], half_rs.at[j], (other, col))

    own_root.wait()
    all_arrived(0)

    def lat_copy(h, j, q, slot):
        return copy(
            lat_out.at[h, q], lat_in.at[h, slot], lat_ss.at[h, j], lat_rs.at[h, j], p_dev(q)
        )

    def send_latent(h):
        def body(i):
            pair = (y + 4 - i) % 4
            if h == 0:

                @pl.when(i > 0)
                def _():
                    share_root(2 * i)

                share_root(2 * i + 1)

                @pl.when(i > 0)
                def _():
                    share_copy(2 * i, other_half).wait_recv()

                share_copy(2 * i + 1, other_half).wait_recv()
            block = rootb[:, :, pl.ds(pl.multiple_of(pair * 256, 256), 256)].reshape(1024, 256)
            piece = lax.dot_general(
                block, projb[h].reshape(1024, N), (((0,), (0,)), ((), ())),
                preferred_element_type=F32,
            )
            lat_out[h, pl.ds(pair * 2, 2)] = piece.reshape(2, 128, N)
            ahead = ((4 - i) % 4) * 2

            @pl.when(i > 0)
            def _():
                lat_copy(h, ahead, p_to(ahead), p).start()

            lat_copy(h, ahead + 1, p_to(ahead + 1), p).start()

        loop(0, 4, body)
        lat_in[h, p] = lat_out[h, p]

    def az_copy(h, j, q, slot):
        return copy(ar_src.at[h], ar_z.at[h, slot], az_ss.at[h, j], az_rs.at[h, j], z_dev(q))

    def ap_copy(h, j, q, slot):
        return copy(ar_p_src.at[h], ar_p.at[h, slot], ap_ss.at[h, j], ap_rs.at[h, j], p_dev(q))

    def sum_latent(h):
        def body(j):
            q = p_from(j)
            lat_copy(h, j, q, q).wait_recv()

        loop(1, 8, body)
        latent = lat_in[h, 0]
        for i in range(1, 8):
            latent = latent + lat_in[h, i]
        lat_in[h, 0] = latent
        ar_src[h, :, :N] = jnp.sum(latent * latent, axis=0, keepdims=True)
        loop(1, 8, lambda j: az_copy(h, j, z_to(j), z).start())
        ar_z[h, z] = ar_src[h]

    def sum_along_z(h):
        loop(1, 8, lambda j: az_copy(h, j, z_from(j), z_from(j)).wait_recv())
        total = ar_z[h, 0]
        for i in range(1, 8):
            total = total + ar_z[h, i]
        ar_p_src[h] = total
        loop(1, 8, lambda j: ap_copy(h, j, p_to(j), p).start())
        ar_p[h, p] = total

    def w_copy(h, j, q, slot):
        return copy(wb.at[h, p], wb.at[h, slot], w_ss.at[h, j], w_rs.at[h, j], p_dev(q))

    def send_weighted(h):
        loop(1, 8, lambda j: ap_copy(h, j, p_from(j), p_from(j)).wait_recv())
        total = ar_p[h, 0]
        for i in range(1, 8):
            total = total + ar_p[h, i]
        rows_ = slice(h * N, (h + 1) * N)
        post_var = resid[:, rows_] + total[:, :N]
        slope_mean, slope_var = slopes(observed[:, rows_], total[:, N:], post_var)
        wb[h, p] = (2.0 * slope_var * lat_in[h, 0]).astype(BF16)
        loop(1, 8, lambda j: w_copy(h, j, p_to(j), p).start())
        return slope_mean

    def x_copy(h, j, q):
        return copy(wb.at[h, q], wx.at[h, q], x_ss.at[h, j], x_rs.at[h, j], (other, col))

    def hand_on(h):
        def body(j):
            q = p_from(j)
            w_copy(h, j, q, q).wait_recv()
            x_copy(h, j, q).start()

        x_copy(h, 0, p).start()
        loop(1, 8, body)

    def root_pair(h, i):
        pair = (y + 4 - i) % 4
        x_copy(h, 2 * i, p_from(2 * i)).wait_recv()
        x_copy(h, 2 * i + 1, p_from(2 * i + 1)).wait_recv()
        both = pl.ds(pair * 2, 2)
        mine = lax.dot_general(
            projb[h, half].reshape(512, N), wb[h, both].reshape(256, N),
            (((1,), (1,)), ((), ())), preferred_element_type=F32,
        )
        return mine + lax.dot_general(
            projx[h].reshape(512, N), wx[h, both].reshape(256, N),
            (((1,), (1,)), ((), ())), preferred_element_type=F32,
        )

    def root_first():
        def body(i):
            grp[i] = root_pair(0, i)

        loop(0, 4, body)

    def m_copy(i, pair, slot):
        return copy(
            gout.at[pl.ds(pair * 2, 2)], mid.at[slot], m_ss.at[i], m_rs.at[slot],
            p_dev(pair * 2 + xh),
        )

    def root_last():
        def body(i):
            piece = root_pair(NH - 1, i)
            if NH == 2:
                piece = piece + grp[i]
            pair = (y + 4 - i) % 4
            left, right = piece[:, :128].astype(BF16), piece[:, 128:].astype(BF16)

            @pl.when(i > 0)
            def _():
                gout[pair * 2] = left
                gout[pair * 2 + 1] = right
                m_copy(i, pair, y).start()

            @pl.when(i == 0)
            def _():
                mid[y, 0] = left
                mid[y, 1] = right

        loop(0, 4, body)

    def g_copy(ys, b):
        return copy(
            mid.at[ys, b], gin.at[me_gr], g_ss.at[ys * 2 + b], g_rs.at[me_gr],
            (ys, column(y, z, b)),
        )

    def to_owners():
        def body(t):
            ys = (y + t) % 4

            @pl.when(t > 0)
            def _():
                m_copy(t, ys, ys).wait_recv()

            for b in range(2):
                mine = jnp.logical_and(ys == d, xh == b)

                @pl.when(mine)
                def _():
                    pltpu.make_async_copy(mid.at[ys, b], gin.at[me_gr], g_rs.at[me_gr]).start()

                @pl.when(jnp.logical_not(mine))
                def _():
                    g_copy(ys, b).start()

        loop(0, 4, body)

    def gp_copy(h, j, q, slot):
        return copy(gpo.at[h, q], gpi.at[h, slot], gp_ss.at[h, j], gp_rs.at[h, j], z_dev(q))

    def proj_pieces(h):
        def body(i):
            base = ((z // 4 + 1 + i) % 2) * 4
            four = pl.ds(base, 4)
            piece = jnp.dot(
                rootb[four].reshape(512, 1024), wb[h].reshape(1024, N),
                preferred_element_type=F32,
            )
            gpo[h, four] = piece.astype(BF16).reshape(4, 128, N)
            for k in range(4):
                q = base + k

                @pl.when(q != z)
                def _():
                    gp_copy(h, (q + 8 - z) % 8, q, z).start()

        loop(0, 2, body)

    def proj_piece(h, q):
        return jnp.dot(rootb[q], wb[h].reshape(1024, N), preferred_element_type=F32)

    if NH == 1:
        all_arrived(1)
        px_copy = copy(projb.at[:, other_half], projx, px_ss, px_rs, (other, col))
        px_copy.start()
        send_latent(0)
        sum_latent(0)
        sum_along_z(0)
        slope_mean = send_weighted(0)
        px_copy.wait_recv()
    else:
        send_latent(0)
        all_arrived(1)
        send_latent(1)
        px_copy = copy(projb.at[:, other_half], projx, px_ss, px_rs, (other, col))
        px_copy.start()
        sum_latent(0)
        sum_along_z(0)
        early = send_weighted(0)
        sum_latent(1)
        sum_along_z(1)
        hand_on(0)
        second = send_weighted(1)
        px_copy.wait_recv()
        proj_pieces(0)
        root_first()
        slope_mean = jnp.concatenate([early, second], axis=1)

    gm = lax.dot_general(
        jnp.broadcast_to(slope_mean, (8, 512)), proj[...].astype(F32),
        (((1,), (1,)), ((), ())), precision=HIGHEST, preferred_element_type=F32,
    )
    gm_src[...] = gm[0:1]
    gm_in[d] = gm[0:1]

    def gm_copy(j, e, slot):
        return copy(gm_src, gm_in.at[slot], gm_ss.at[j], gm_rs.at[j], (e, col))

    loop(1, 4, lambda j: gm_copy(j, (d + j) % 4, d).start())
    hand_on(NH - 1)
    proj_pieces(NH - 1)
    root_last()
    to_owners()

    for way in (1, -1):
        for c in range(2):
            for dist in range(1, 5):
                if goes(way, dist, c):
                    (first if dist < 3 else onward)(way, dist, c).wait_send()

    def drain(j):
        root_copy(j).wait_send()
        share_copy(j, half).wait_send()
        for h in range(NH):
            lat_copy(h, j, p_to(j), p).wait_send()
            az_copy(h, j, z_to(j), z).wait_send()
            ap_copy(h, j, p_to(j), p).wait_send()
            w_copy(h, j, p_to(j), p).wait_send()
            x_copy(h, j, p_from(j)).wait_send()

    loop(1, 8, drain)
    loop(1, 4, lambda j: gm_copy(j, (d + j) % 4, d).wait_send())

    px_copy.wait_send()
    for h in range(NH):
        x_copy(h, 0, p).wait_send()

    outer = jnp.transpose(mean_rows)[:, 0:1] * slope_mean
    for h in range(NH):
        lat_in[h, 1] = proj_piece(h, z) + outer[:, h * N : (h + 1) * N]
    loop(1, 4, lambda j: gm_copy(j, (d + 4 - j) % 4, (d + 4 - j) % 4).wait_recv())
    out_mean[...] = gm_in[0] + gm_in[1] + gm_in[2] + gm_in[3]

    for h in range(NH):

        def add_gp(j):
            q = z_from(j)
            gp_copy(h, j, q, q).wait_recv()
            lat_in[h, 1] += gpi[h, q].astype(F32)

        loop(1, 8, add_gp)
        out_proj[:, h * N : (h + 1) * N] = lat_in[h, 1]

    def wait_gr(s):
        pltpu.make_async_copy(gin.at[s], gin.at[s], g_rs.at[s]).wait()

    loop(0, 8, wait_gr)
    for k in range(2):
        for h in range(2):
            block = gin[k * 2 + h].astype(F32) + gin[4 + k * 2 + h].astype(F32)
            out_root[k * 4 : k * 4 + 4, h] = block.reshape(4, 128, 128)

    for h in range(NH):
        loop(1, 8, lambda j: gp_copy(h, j, z_to(j), z).wait_send())
    loop(1, 4, lambda i: m_copy(i, (y + 4 - i) % 4, y).wait_send())

    def drain_gr(ys):
        for b in range(2):

            @pl.when(jnp.logical_not(jnp.logical_and(ys == d, xh == b)))
            def _():
                g_copy(ys, b).wait_send()

    loop(0, 4, drain_gr)


def on_device(proj, mean, root, resid_var, targets, indices):
    vmem = pl.BlockSpec(memory_space=pltpu.VMEM)
    hbm = pl.BlockSpec(memory_space=pltpu.HBM)
    sem = pltpu.SemaphoreType.DMA
    out_mean, out_root, out_proj = pl.pallas_call(
        kernel,
        out_shape=(
            jax.ShapeDtypeStruct((1, 128), F32),
            jax.ShapeDtypeStruct((8, 2, 128, 128), F32),
            jax.ShapeDtypeStruct((128, 512), F32),
        ),
        in_specs=[hbm] * 6,
        out_specs=(vmem, vmem, vmem),
        scratch_shapes=[
            pltpu.VMEM((128, 512), BF16),
            pltpu.VMEM((1, 128), F32),
            pltpu.VMEM((1, 512), F32),
            pltpu.VMEM((512, 128), F32),
            pltpu.VMEM((1, 512), jnp.int32),
            sem((5,)),
            pltpu.VMEM((8, 128, 1024), BF16),
            pltpu.VMEM((NH, 8, 128, N), BF16),
            pltpu.VMEM((NH, 4, 128, N), BF16),
            pltpu.VMEM((NH, 8, 128, N), F32),
            pltpu.VMEM((NH, 8, 128, N), F32),
            pltpu.VMEM((NH, 8, 128, N), BF16),
            pltpu.VMEM((NH, 8, 128, N), BF16),
            pltpu.VMEM((4, 512, 256), F32),
            pltpu.VMEM((8, 512, 128), BF16),
            pltpu.VMEM((4, 2, 512, 128), BF16),
            pltpu.VMEM((8, 512, 128), BF16),
            pltpu.VMEM((NH, 8, 128, N), BF16),
            pltpu.VMEM((NH, 8, 128, N), BF16),
            pltpu.VMEM((NH, 1, 2 * N), F32),
            pltpu.VMEM((NH, 8, 1, 2 * N), F32),
            pltpu.VMEM((NH, 1, 2 * N), F32),
            pltpu.VMEM((NH, 8, 1, 2 * N), F32),
            pltpu.VMEM((1, 128), F32),
            pltpu.VMEM((4, 1, 128), F32),
            sem,
            sem((8,)), sem((8,)), sem((8,)), sem((8,)),
            sem((4, 5)), sem((4, 5)),
            sem((NH, 8)), sem((NH, 8)), sem((NH, 8)), sem((NH, 8)),
            sem((NH, 8)), sem((NH, 8)), sem((NH, 8)), sem((NH, 8)),
            sem, sem, sem((NH, 8)), sem((NH, 8)), sem((4,)), sem((4,)), sem((8,)), sem((8,)),
            sem((NH, 8)), sem((NH, 8)), sem((4,)), sem((4,)),
        ],
        compiler_params=pltpu.CompilerParams(
            collective_id=0, has_side_effects=True, vmem_limit_bytes=62 * 2**20
        ),
    )(
        proj,
        mean.reshape(1, 128),
        root.reshape(4, 8, 2, 128, 128),
        resid_var.reshape(1, 512),
        targets.reshape(512, 128),
        indices.reshape(1, 512),
    )
    return out_mean.reshape(128), out_root.reshape(2048, 128), out_proj


def solution(mesh):
    return jax.shard_map(
        on_device,
        mesh=mesh,
        in_specs=(P("col", "dp"), P("col"), P(None, "col"), P("dp"), P(), P("dp")),
        out_specs=(P("col"), P("dp", "col"), P("col", "dp")),
        check_vma=False,
    )
```

```python
import functools

import jax
import jax.numpy as jnp
import numpy as np
from jax import lax
from jax.experimental import pallas as pl
from jax.experimental.pallas import tpu as pltpu
from jax.sharding import PartitionSpec as P

WINDOW = 65536
ROWS = 2048
MESH = pl.DeviceIdType.MESH
NH = 2
N = 512 // NH
F32 = jnp.float32
BF16 = jnp.bfloat16
HIGHEST = lax.Precision.HIGHEST

freedom = 4.0
half_knots = [
    0.2453407083009012,
    0.7374737285453944,
    1.234076215395323,
    1.7385377121165861,
    2.2549740020892757,
    2.7888060584281305,
    3.3478545673832163,
    3.944764040115625,
    4.603682449550744,
    5.387480890011233,
]
half_weights = [
    0.4622436696006101,
    0.2866755053628341,
    0.1090172060200233,
    0.024810520887463612,
    0.0032437733422378567,
    0.00022833863601635319,
    7.802556478532063e-06,
    1.0860693707692819e-07,
    4.3993409922731804e-10,
    2.2293936455341508e-13,
]


def slopes(observed, post_mean, post_var):
    knots = [-k for k in half_knots[::-1]] + half_knots
    weights = half_weights[::-1] + half_weights
    spread_root = jnp.sqrt(2.0 * post_var)
    total_mean = jnp.zeros_like(observed)
    total_var = jnp.zeros_like(observed)
    for knot, weight in zip(knots, weights):
        knot = float(np.float32(knot))
        weight = float(np.float32(weight / np.sqrt(np.pi)))
        gap = observed - (post_mean + spread_root * knot)
        term = weight * ((freedom + 1.0) * gap / (freedom + gap * gap))
        total_mean = total_mean + term
        total_var = total_var + term * knot
    factor = WINDOW / ROWS
    return factor * total_mean, factor * total_var / spread_root


def kernel(
    proj_hbm, mean_hbm, root, resid_hbm, table_hbm, index_hbm,
    out_mean, out_root, out_proj,
    proj, mean, resid, table, index, in_sem,
    rootb, projb, projx, lat_out, lat_in, wb, wx, grp, gout, mid, gin, gpo, gpi,
    ar_src, ar_z, ar_p_src, ar_p, gm_src, gm_in,
    local_sem, root_ss, root_rs, half_ss, half_rs, z_ss, z_rs,
    lat_ss, lat_rs, az_ss, az_rs, ap_ss, ap_rs, w_ss, w_rs,
    px_ss, px_rs, x_ss, x_rs, m_ss, m_rs, g_ss, g_rs, gp_ss, gp_rs, gm_ss, gm_rs,
):
    d = lax.axis_index("dp")
    col = lax.axis_index("col")
    core = d % 2
    y, z, xh = col // 16, (col // 2) % 8, col % 2
    p = y * 2 + xh
    other = d + 1 - 2 * core

    def column(y_, z_, xh_):
        return y_ * 16 + z_ * 2 + xh_

    def p_to(j):
        return ((y + j // 2) % 4) * 2 + (xh + j % 2) % 2

    def p_from(j):
        return ((y + 4 - j // 2) % 4) * 2 + (xh + 2 - j % 2) % 2

    def p_dev(q):
        return (d, column(q // 2, z, q % 2))

    def z_to(j):
        return (z + j) % 8

    def z_from(j):
        return (z + 8 - j) % 8

    def z_dev(q):
        return (d, column(y, q, xh))

    def copy(src, dst, ss, rs, dev):
        return pltpu.make_async_remote_copy(
            src_ref=src, dst_ref=dst, send_sem=ss, recv_sem=rs,
            device_id=dev, device_id_type=MESH,
        )

    def loop(lo, hi, body):
        def step(j, carry):
            body(j)
            return carry
        lax.fori_loop(lo, hi, step, 0)

    incoming = [
        pltpu.make_async_copy(a, b, in_sem.at[i])
        for i, (a, b) in enumerate(
            [
                (proj_hbm, proj), (mean_hbm, mean), (index_hbm, index),
                (table_hbm, table), (resid_hbm, resid),
            ]
        )
    ]
    for item in incoming:
        item.start()

    def cols(q):
        return pl.ds(pl.multiple_of(q * 128, 128), 128)

    own_root = pltpu.make_async_copy(root.at[y, :, xh], rootb.at[:, :, cols(p)], local_sem)
    own_root.start()

    me_gr = d * 2 + xh

    barrier = pltpu.get_barrier_semaphore()

    def greet(dev):
        pl.semaphore_signal(barrier, inc=1, device_id=dev, device_id_type=MESH)

    for j in (1, 2):
        greet(z_dev(z_to(j)))
        greet(z_dev(z_from(j)))
    loop(1, 8, lambda j: greet(p_dev(p_from(j))))
    loop(1, 4, lambda j: greet(((d + j) % 4, col)))
    pl.semaphore_wait(barrier, 4 + 7 + 3)

    def part(zz, c):
        if NH == 2:
            return projb.at[c, zz]
        return projb.at[0, zz, :, c * 256 : (c + 1) * 256]

    def first(way, dist, c):
        i = (0 if way == 1 else 1) * 2 + c
        block = part(z, c)
        return copy(block, block, z_ss.at[i, dist], z_rs.at[i, dist], z_dev((z + 8 + way * dist) % 8))

    def onward(way, dist, c):
        i = (0 if way == 1 else 1) * 2 + c
        block = part((z + 8 - way * 2) % 8, c)
        return copy(block, block, z_ss.at[i, dist], z_rs.at[i, dist], z_dev((z + 8 + way * (dist - 2)) % 8))

    def goes(way, dist, c):
        return dist < 4 or (c == 0) == (way == 1)

    def arrived(way, dist, c):
        i = (0 if way == 1 else 1) * 2 + c
        block = part((z + 8 - way * dist) % 8, c)
        copy(block, block, z_ss.at[i, dist], z_rs.at[i, dist], z_dev((z + 8 + way) % 8)).wait_recv()

    def send_first(c):
        for dist in (2, 1):
            for way in (1, -1):
                first(way, dist, c).start()

    def send_onward(c):
        for way in (1, -1):
            arrived(way, 2, c)
            for dist in (4, 3):
                if goes(way, dist, c):
                    onward(way, dist, c).start()

    def all_arrived(c):
        for dist in (1, 3, 4):
            for way in (1, -1):
                if goes(way, dist, c):
                    arrived(way, dist, c)

    half = pl.ds(core * 4, 4)
    other_half = pl.ds((1 - core) * 4, 4)

    def root_copy(j):
        q = p_to(j)
        return copy(
            root.at[q // 2, half, q % 2], rootb.at[half, :, cols(p)],
            root_ss.at[j], root_rs.at[j], p_dev(q),
        )

    incoming[0].wait()
    for h in range(NH):
        projb[h, z] = proj[:, h * N : (h + 1) * N]
    send_first(0)
    loop(1, 8, lambda j: root_copy(j).start())
    send_first(1)
    for item in incoming[1:]:
        item.wait()

    mean_rows = jnp.broadcast_to(mean[...], (8, 128))
    part_mean = jnp.dot(
        mean_rows, proj[...].astype(F32), precision=HIGHEST, preferred_element_type=F32
    )
    for h in range(NH):
        ar_src[h, :, N:] = part_mean[0:1, h * N : (h + 1) * N]
    send_onward(0)
    picked = []
    for i in range(4):
        idx = index[:, i * 128 : (i + 1) * 128]
        row, lane = idx // 128, idx % 128
        chosen = jnp.where(lax.broadcasted_iota(jnp.int32, (512, 128), 0) == row, 1.0, 0.0)
        values = lax.dot_general(
            table[...], chosen, (((0,), (0,)), ((), ())),
            precision=HIGHEST, preferred_element_type=F32,
        )
        here = lax.broadcasted_iota(jnp.int32, (128, 128), 0) == lane
        picked.append(jnp.sum(jnp.where(here, values, 0.0), axis=0, keepdims=True))
    observed = jnp.concatenate(picked, axis=1)

    send_onward(1)

    def share_root(j):
        q = p_from(j)
        copy(
            root.at[y, half, xh], rootb.at[half, :, cols(q)],
            root_ss.at[j], root_rs.at[j], p_dev(q),
        ).wait_recv()
        share_copy(j, half).start()

    def share_copy(j, rows_):
        block = rootb.at[rows_, :, cols(p_from(j))]
        return copy(block, block, half_ss.at[j], half_rs.at[j], (other, col))

    own_root.wait()
    all_arrived(0)

    def lat_copy(h, j, q, slot):
        return copy(
            lat_out.at[h, q], lat_in.at[h, slot], lat_ss.at[h, j], lat_rs.at[h, j], p_dev(q)
        )

    def send_latent(h):
        def body(i):
            pair = (y + 4 - i) % 4
            if h == 0:

                @pl.when(i > 0)
                def _():
                    share_root(2 * i)

                share_root(2 * i + 1)

                @pl.when(i > 0)
                def _():
                    share_copy(2 * i, other_half).wait_recv()

                share_copy(2 * i + 1, other_half).wait_recv()
            block = rootb[:, :, pl.ds(pl.multiple_of(pair * 256, 256), 256)].reshape(1024, 256)
            piece = lax.dot_general(
                block, projb[h].reshape(1024, N), (((0,), (0,)), ((), ())),
                preferred_element_type=F32,
            )
            lat_out[h, pl.ds(pair * 2, 2)] = piece.reshape(2, 128, N)
            ahead = ((4 - i) % 4) * 2

            @pl.when(i > 0)
            def _():
                lat_copy(h, ahead, p_to(ahead), p).start()

            lat_copy(h, ahead + 1, p_to(ahead + 1), p).start()

        loop(0, 4, body)
        lat_in[h, p] = lat_out[h, p]

    def az_copy(h, j, q, slot):
        return copy(ar_src.at[h], ar_z.at[h, slot], az_ss.at[h, j], az_rs.at[h, j], z_dev(q))

    def ap_copy(h, j, q, slot):
        return copy(ar_p_src.at[h], ar_p.at[h, slot], ap_ss.at[h, j], ap_rs.at[h, j], p_dev(q))

    def sum_latent(h):
        def body(j):
            q = p_from(j)
            lat_copy(h, j, q, q).wait_recv()

        loop(1, 8, body)
        latent = lat_in[h, 0]
        for i in range(1, 8):
            latent = latent + lat_in[h, i]
        lat_in[h, 0] = latent
        ar_src[h, :, :N] = jnp.sum(latent * latent, axis=0, keepdims=True)
        loop(1, 8, lambda j: az_copy(h, j, z_to(j), z).start())
        ar_z[h, z] = ar_src[h]

    def sum_along_z(h):
        loop(1, 8, lambda j: az_copy(h, j, z_from(j), z_from(j)).wait_recv())
        total = ar_z[h, 0]
        for i in range(1, 8):
            total = total + ar_z[h, i]
        ar_p_src[h] = total
        loop(1, 8, lambda j: ap_copy(h, j, p_to(j), p).start())
        ar_p[h, p] = total

    def w_copy(h, j, q, slot):
        return copy(wb.at[h, p], wb.at[h, slot], w_ss.at[h, j], w_rs.at[h, j], p_dev(q))

    def send_weighted(h):
        loop(1, 8, lambda j: ap_copy(h, j, p_from(j), p_from(j)).wait_recv())
        total = ar_p[h, 0]
        for i in range(1, 8):
            total = total + ar_p[h, i]
        rows_ = slice(h * N, (h + 1) * N)
        post_var = resid[:, rows_] + total[:, :N]
        slope_mean, slope_var = slopes(observed[:, rows_], total[:, N:], post_var)
        wb[h, p] = (2.0 * slope_var * lat_in[h, 0]).astype(BF16)
        loop(1, 8, lambda j: w_copy(h, j, p_to(j), p).start())
        return slope_mean

    def x_copy(h, j, q):
        return copy(wb.at[h, q], wx.at[h, q], x_ss.at[h, j], x_rs.at[h, j], (other, col))

    def hand_on(h):
        def body(j):
            q = p_from(j)
            w_copy(h, j, q, q).wait_recv()
            x_copy(h, j, q).start()

        x_copy(h, 0, p).start()
        loop(1, 8, body)

    def root_pair(h, i):
        pair = (y + 4 - i) % 4
        x_copy(h, 2 * i, p_from(2 * i)).wait_recv()
        x_copy(h, 2 * i + 1, p_from(2 * i + 1)).wait_recv()
        both = pl.ds(pair * 2, 2)
        mine = lax.dot_general(
            projb[h, half].reshape(512, N), wb[h, both].reshape(256, N),
            (((1,), (1,)), ((), ())), preferred_element_type=F32,
        )
        return mine + lax.dot_general(
            projx[h].reshape(512, N), wx[h, both].reshape(256, N),
            (((1,), (1,)), ((), ())), preferred_element_type=F32,
        )

    def root_first():
        def body(i):
            grp[i] = root_pair(0, i)

        loop(0, 4, body)

    def m_copy(i, pair, slot):
        return copy(
            gout.at[pl.ds(pair * 2, 2)], mid.at[slot], m_ss.at[i], m_rs.at[slot],
            p_dev(pair * 2 + xh),
        )

    def root_last():
        def body(i):
            piece = root_pair(NH - 1, i)
            if NH == 2:
                piece = piece + grp[i]
            pair = (y + 4 - i) % 4
            left, right = piece[:, :128].astype(BF16), piece[:, 128:].astype(BF16)

            @pl.when(i > 0)
            def _():
                gout[pair * 2] = left
                gout[pair * 2 + 1] = right
                m_copy(i, pair, y).start()

            @pl.when(i == 0)
            def _():
                mid[y, 0] = left
                mid[y, 1] = right

        loop(0, 4, body)

    def g_copy(ys, b):
        return copy(
            mid.at[ys, b], gin.at[me_gr], g_ss.at[ys * 2 + b], g_rs.at[me_gr],
            (ys, column(y, z, b)),
        )

    def to_owners():
        def body(t):
            ys = (y + t) % 4

            @pl.when(t > 0)
            def _():
                m_copy(t, ys, ys).wait_recv()

            for b in range(2):
                mine = jnp.logical_and(ys == d, xh == b)

                @pl.when(mine)
                def _():
                    pltpu.make_async_copy(mid.at[ys, b], gin.at[me_gr], g_rs.at[me_gr]).start()

                @pl.when(jnp.logical_not(mine))
                def _():
                    g_copy(ys, b).start()

        loop(0, 4, body)

    def gp_copy(h, j, q, slot):
        return copy(gpo.at[h, q], gpi.at[h, slot], gp_ss.at[h, j], gp_rs.at[h, j], z_dev(q))

    def proj_pieces(h):
        def body(i):
            base = ((z // 4 + 1 + i) % 2) * 4
            four = pl.ds(base, 4)
            piece = jnp.dot(
                rootb[four].reshape(512, 1024), wb[h].reshape(1024, N),
                preferred_element_type=F32,
            )
            gpo[h, four] = piece.astype(BF16).reshape(4, 128, N)
            for k in range(4):
                q = base + k

                @pl.when(q != z)
                def _():
                    gp_copy(h, (q + 8 - z) % 8, q, z).start()

        loop(0, 2, body)

    def proj_piece(h, q):
        return jnp.dot(rootb[q], wb[h].reshape(1024, N), preferred_element_type=F32)

    if NH == 1:
        all_arrived(1)
        px_copy = copy(projb.at[:, other_half], projx, px_ss, px_rs, (other, col))
        px_copy.start()
        send_latent(0)
        sum_latent(0)
        sum_along_z(0)
        slope_mean = send_weighted(0)
        px_copy.wait_recv()
    else:
        send_latent(0)
        all_arrived(1)
        send_latent(1)
        sum_latent(0)
        sum_along_z(0)
        early = send_weighted(0)
        px_copy = copy(projb.at[:, other_half], projx, px_ss, px_rs, (other, col))
        px_copy.start()
        sum_latent(1)
        sum_along_z(1)
        second = send_weighted(1)
        hand_on(0)
        px_copy.wait_recv()
        proj_pieces(0)
        root_first()
        slope_mean = jnp.concatenate([early, second], axis=1)

    gm = lax.dot_general(
        jnp.broadcast_to(slope_mean, (8, 512)), proj[...].astype(F32),
        (((1,), (1,)), ((), ())), precision=HIGHEST, preferred_element_type=F32,
    )
    gm_src[...] = gm[0:1]
    gm_in[d] = gm[0:1]

    def gm_copy(j, e, slot):
        return copy(gm_src, gm_in.at[slot], gm_ss.at[j], gm_rs.at[j], (e, col))

    loop(1, 4, lambda j: gm_copy(j, (d + j) % 4, d).start())
    hand_on(NH - 1)
    proj_pieces(NH - 1)
    root_last()
    to_owners()

    for way in (1, -1):
        for c in range(2):
            for dist in range(1, 5):
                if goes(way, dist, c):
                    (first if dist < 3 else onward)(way, dist, c).wait_send()

    def drain(j):
        root_copy(j).wait_send()
        share_copy(j, half).wait_send()
        for h in range(NH):
            lat_copy(h, j, p_to(j), p).wait_send()
            az_copy(h, j, z_to(j), z).wait_send()
            ap_copy(h, j, p_to(j), p).wait_send()
            w_copy(h, j, p_to(j), p).wait_send()
            x_copy(h, j, p_from(j)).wait_send()

    loop(1, 8, drain)
    loop(1, 4, lambda j: gm_copy(j, (d + j) % 4, d).wait_send())

    px_copy.wait_send()
    for h in range(NH):
        x_copy(h, 0, p).wait_send()

    outer = jnp.transpose(mean_rows)[:, 0:1] * slope_mean
    for h in range(NH):
        lat_in[h, 1] = proj_piece(h, z) + outer[:, h * N : (h + 1) * N]
    loop(1, 4, lambda j: gm_copy(j, (d + 4 - j) % 4, (d + 4 - j) % 4).wait_recv())
    out_mean[...] = gm_in[0] + gm_in[1] + gm_in[2] + gm_in[3]

    for h in range(NH):

        def add_gp(j):
            q = z_from(j)
            gp_copy(h, j, q, q).wait_recv()
            lat_in[h, 1] += gpi[h, q].astype(F32)

        loop(1, 8, add_gp)
        out_proj[:, h * N : (h + 1) * N] = lat_in[h, 1]

    def wait_gr(s):
        pltpu.make_async_copy(gin.at[s], gin.at[s], g_rs.at[s]).wait()

    loop(0, 8, wait_gr)
    for s_ in range(8):
        a, k, b = s_ // 4, (s_ // 2) % 2, s_ % 2
        out_root[a, k * 4 : k * 4 + 4, b] = gin[s_].reshape(4, 128, 128)

    for h in range(NH):
        loop(1, 8, lambda j: gp_copy(h, j, z_to(j), z).wait_send())
    loop(1, 4, lambda i: m_copy(i, (y + 4 - i) % 4, y).wait_send())

    def drain_gr(ys):
        for b in range(2):

            @pl.when(jnp.logical_not(jnp.logical_and(ys == d, xh == b)))
            def _():
                g_copy(ys, b).wait_send()

    loop(0, 4, drain_gr)


def on_device(proj, mean, root, resid_var, targets, indices):
    vmem = pl.BlockSpec(memory_space=pltpu.VMEM)
    hbm = pl.BlockSpec(memory_space=pltpu.HBM)
    sem = pltpu.SemaphoreType.DMA
    out_mean, out_root, out_proj = pl.pallas_call(
        kernel,
        out_shape=(
            jax.ShapeDtypeStruct((1, 128), F32),
            jax.ShapeDtypeStruct((2, 8, 2, 128, 128), BF16),
            jax.ShapeDtypeStruct((128, 512), F32),
        ),
        in_specs=[hbm] * 6,
        out_specs=(vmem, vmem, vmem),
        scratch_shapes=[
            pltpu.VMEM((128, 512), BF16),
            pltpu.VMEM((1, 128), F32),
            pltpu.VMEM((1, 512), F32),
            pltpu.VMEM((512, 128), F32),
            pltpu.VMEM((1, 512), jnp.int32),
            sem((5,)),
            pltpu.VMEM((8, 128, 1024), BF16),
            pltpu.VMEM((NH, 8, 128, N), BF16),
            pltpu.VMEM((NH, 4, 128, N), BF16),
            pltpu.VMEM((NH, 8, 128, N), F32),
            pltpu.VMEM((NH, 8, 128, N), F32),
            pltpu.VMEM((NH, 8, 128, N), BF16),
            pltpu.VMEM((NH, 8, 128, N), BF16),
            pltpu.VMEM((4, 512, 256), F32),
            pltpu.VMEM((8, 512, 128), BF16),
            pltpu.VMEM((4, 2, 512, 128), BF16),
            pltpu.VMEM((8, 512, 128), BF16),
            pltpu.VMEM((NH, 8, 128, N), BF16),
            pltpu.VMEM((NH, 8, 128, N), BF16),
            pltpu.VMEM((NH, 1, 2 * N), F32),
            pltpu.VMEM((NH, 8, 1, 2 * N), F32),
            pltpu.VMEM((NH, 1, 2 * N), F32),
            pltpu.VMEM((NH, 8, 1, 2 * N), F32),
            pltpu.VMEM((1, 128), F32),
            pltpu.VMEM((4, 1, 128), F32),
            sem,
            sem((8,)), sem((8,)), sem((8,)), sem((8,)),
            sem((4, 5)), sem((4, 5)),
            sem((NH, 8)), sem((NH, 8)), sem((NH, 8)), sem((NH, 8)),
            sem((NH, 8)), sem((NH, 8)), sem((NH, 8)), sem((NH, 8)),
            sem, sem, sem((NH, 8)), sem((NH, 8)), sem((4,)), sem((4,)), sem((8,)), sem((8,)),
            sem((NH, 8)), sem((NH, 8)), sem((4,)), sem((4,)),
        ],
        compiler_params=pltpu.CompilerParams(
            collective_id=0, has_side_effects=True, vmem_limit_bytes=62 * 2**20
        ),
    )(
        proj,
        mean.reshape(1, 128),
        root.reshape(4, 8, 2, 128, 128),
        resid_var.reshape(1, 512),
        targets.reshape(512, 128),
        indices.reshape(1, 512),
    )
    shares = out_root.reshape(2, 2048, 128).astype(F32)
    grad_root = shares[0] + shares[1]
    return out_mean.reshape(128), grad_root, out_proj


def solution(mesh):
    return jax.shard_map(
        on_device,
        mesh=mesh,
        in_specs=(P("col", "dp"), P("col"), P(None, "col"), P("dp"), P(), P("dp")),
        out_specs=(P("col"), P("dp", "col"), P("col", "dp")),
        check_vma=False,
    )
```
